32 devices in a mesh: stream: 4 (over y, x), span: 8 (over z, core).
Axes of the slice: x: 2, y: 2, z: 4, core: 2. Of those that a mesh axis runs over, the one named last changes fastest.
Arguments:
- forcing: float32 [5, 256, 128, 128], P(None, 'span', 'stream'), may hold values from -6 to 6
- initial_state: float32 [128, 5, 2, 128, 128], P('span', None, None, 'stream'), may hold values from -4 to 4
- diagonal: float32 [5, 128, 128], replicated, may hold values from 1.5 to 4
- span_speed: float32 [5], replicated, may hold values from 0.3 to 3
- coupling: float32 [4, 5, 5], replicated, may hold values from -1.25 to 1.25
- stiffener_mask: int32 [128, 128], replicated, may hold values 0 or 1
- face_index: int32 [2, 4096], P(None, ('stream', 'span')), may hold values from 0 to 1023
- mode_shapes: float32 [2, 2, 4096], P(None, None, ('stream', 'span')), may hold values from -12 to 12
Outputs:
- flow: float32 [128, 5, 2, 128, 128], P('span', None, None, 'stream')
- forces: float32 [2, 2], replicated
The draws below stay inside these ranges and needn't reach their ends.
All inputs are finite; a program needn't handle non-finite values.
Results may differ from the reference program's by a relative error of at most 0.00025.
Values sent between devices are 32-bit elements; how exact they have to be, the bound alone decides.
No kernel may reach another device: no remote copies, remote signals or barrier semaphores. Data moves between devices by JAX's collectives and lax.ppermute only.
A program may use at most 192 MiB of HBM per device.

```python
import math
import jax
import jax.numpy as jnp
from jax import lax

C = 5
M = 2
NY = 128
XD = 32
ZD = 32
FACE_DEV = 128
NX = 128
NZ = 256
KW = 128
FACES = 4096
N_SPAN = 8


def draw_mode_shapes(key, part):
    ramp = 1.0 + 2.0 * jnp.arange(FACES, dtype=jnp.float32) / FACES
    base = jnp.clip(jax.random.normal(key, (M, 2, FACES), jnp.float32), -4.0, 4.0)
    return base * ramp


def place_ends(drawn, own_key, smallest, top_value):
    longest = drawn.shape.index(max(drawn.shape))
    spots = []
    for shift in (0, 1):
        where = [jax.random.randint(jax.random.fold_in(own_key, axis), (), 0, length) for axis, length in enumerate(drawn.shape)]
        where[longest] = (where[longest] + shift) % drawn.shape[longest]
        spots.append(tuple(where))
    return drawn.at[spots[0]].set(smallest).at[spots[1]].set(top_value)


def block_levels(rng, shape, split, least, high):
    def one(axis_at, parts):
        heights = jax.random.uniform(jax.random.fold_in(jax.random.fold_in(rng, 6), axis_at), (parts,), jnp.float32, least / len(split), high / len(split))
        return jnp.repeat(jnp.exp(heights), shape[axis_at] // parts).reshape((-1,) + (1,) * (len(shape) - axis_at - 1))

    loudness = one(*split[0])
    for cut in split[1:]:
        loudness = loudness * one(*cut)
    return loudness


def noise(own_key, dims, deviation, limit, pieces=(), held_as=jnp.bfloat16):
    array = jax.random.normal(own_key, dims, jnp.float32) * deviation
    if len(pieces) > 0:
        array = block_levels(own_key, dims, pieces, -0.22, 0.18) * array
    return jnp.clip(array, min=-limit, max=limit).astype(held_as)


def setup_inputs(seed: int = 0) -> dict:
    splits = jax.random.split(jax.random.key(seed), 9)
    return {
        "forcing": noise(splits[0], (C, NZ, NX, NY), 1.0, 6.0, ((1, 8), (2, 4)), jnp.float32),
        "initial_state": noise(splits[1], (KW, C, 2, NX, NY), 0.5, 4.0, ((0, 8), (3, 4)), jnp.float32),
        "diagonal": jnp.clip(jax.random.uniform(splits[2], (C, NX, NY), jnp.float32, 1.5, 4.0), 1.5, 4.0),
        "span_speed": jnp.clip(jnp.exp(jax.random.uniform(splits[3], (C,), jnp.float32, math.log(0.3), math.log(3.0))), 0.3, 3.0),
        "coupling": noise(splits[4], (4, C, C), (4 * C) ** -0.5, 1.25, (), jnp.float32),
        "stiffener_mask": place_ends((jax.random.randint(splits[5], (NX, NY), 0, 8) < 1).astype(jnp.int32), jax.random.fold_in(splits[5], 1), 0, 1),
        "face_index": place_ends(jax.random.randint(splits[6], (M, FACES), 0, XD * ZD), jax.random.fold_in(splits[6], 1), 0, (XD * ZD) - 1).astype(jnp.int32),
        "mode_shapes": draw_mode_shapes(jax.random.fold_in(splits[8], 71), 0),
    }


def wave_table(z_index, k_index, span_total):
    phase_index = z_index[:, None] * k_index[None, :] % span_total
    phase = phase_index.astype(jnp.float32) * (2.0 * math.pi / span_total)
    norm_factor = 1.0 / math.sqrt(span_total)
    return jnp.stack([jnp.cos(phase), -jnp.sin(phase)], axis=-1) * norm_factor

def inverse_table(k_index, z_index, span_total):
    tab = wave_table(z_index, k_index, span_total)
    fold_weight = jnp.where(k_index == 0, 1.0, 2.0).astype(jnp.float32)
    return jnp.transpose(tab, (1, 2, 0)) * fold_weight[:, None, None]

def relax_sweep(state_ext, rhs, diag_part, keep, wavenumber, span_speed, coupling):
    hi = lax.Precision.HIGHEST
    padded = jnp.pad(state_ext, ((0, 0), (0, 0), (0, 0), (0, 0), (1, 1)))
    neighbours = jnp.einsum('cd,kdrxy->kcrxy', coupling[0], padded[:, :, :, 2:, 1:-1], precision=hi)
    neighbours = neighbours + jnp.einsum('cd,kdrxy->kcrxy', coupling[1], padded[:, :, :, :-2, 1:-1], precision=hi)
    neighbours = neighbours + jnp.einsum('cd,kdrxy->kcrxy', coupling[2], padded[:, :, :, 1:-1, 2:], precision=hi)
    neighbours = neighbours + jnp.einsum('cd,kdrxy->kcrxy', coupling[3], padded[:, :, :, 1:-1, :-2], precision=hi)
    defect = rhs - neighbours
    span_part = wavenumber[:, None, None, None] * span_speed[None, :, None, None]
    diag_b = diag_part[None]
    modulus = diag_b * diag_b + span_part * span_part
    real_part = (diag_b * defect[:, :, 0] + span_part * defect[:, :, 1]) / modulus
    imag_part = (diag_b * defect[:, :, 1] - span_part * defect[:, :, 0]) / modulus
    return jnp.stack([real_part, imag_part], axis=2) * keep

def pad_stream(state):
    return jnp.pad(state, ((0, 0), (0, 0), (0, 0), (1, 1), (0, 0)))

def reference(forcing, initial_state, diagonal, span_speed, coupling, stiffener_mask, face_index, mode_shapes):
    hi = lax.Precision.HIGHEST
    z_all = jnp.arange(NZ, dtype=jnp.int32)
    k_all = jnp.arange(KW, dtype=jnp.int32)
    dft_table = wave_table(z_all, k_all, NZ)
    rhs = jnp.einsum('czxy,zkr->kcrxy', forcing, dft_table, precision=hi)
    wavenumber = k_all.astype(jnp.float32) * (2.0 * math.pi / NZ)
    keep = (1 - stiffener_mask).astype(jnp.float32)

    def solve_wave(inputs):
        rhs_one, start_one, wave_one = inputs
        first_pass = relax_sweep(pad_stream(start_one), rhs_one, diagonal, keep, wave_one, span_speed, coupling)
        return relax_sweep(pad_stream(first_pass), rhs_one, diagonal, keep, wave_one, span_speed, coupling)
    flow = lax.map(solve_wave, (rhs[:, None], initial_state[:, None], wavenumber[:, None]))[:, 0]
    wall = flow[:, C - 1, :, :, 0]
    pressure = jnp.einsum('krx,krz->zx', wall, inverse_table(k_all, z_all, NZ), precision=hi)
    face_all = jnp.arange(FACES, dtype=jnp.int32)
    device_of = face_all // FACE_DEV
    stream_of = device_of // N_SPAN
    span_of = device_of % N_SPAN
    z_cell = span_of[None, :] * ZD + face_index // XD
    x_cell = stream_of[None, :] * XD + face_index % XD
    face_values = pressure[z_cell, x_cell]
    forces = lax.optimization_barrier(jnp.sum(face_values[:, None, :] * mode_shapes, axis=-1)) / math.sqrt(FACES)
    return (flow, forces)
```

```python
import functools
import math

import jax
import jax.numpy as jnp
from jax import lax
from jax.experimental import pallas as pl
from jax.experimental.pallas import tpu as pltpu
from jax.sharding import PartitionSpec as P

HI = lax.Precision.HIGHEST


def swap(value, axis, dist):
    count = lax.axis_size(axis)
    return lax.ppermute(value, axis, [(i, i ^ dist) for i in range(count)])


def halo(head, tail, axis):
    ends = lax.axis_size(axis) - 1
    left = lax.ppermute(tail, axis, [(i, i + 1) for i in range(ends)])
    right = lax.ppermute(head, axis, [(i + 1, i) for i in range(ends)])
    return left, right


def wave_rows(owners, blocks, me, waves, cells, span_total):
    k = (jnp.stack([me ^ d for d in owners])[:, None] * waves + jnp.arange(waves, dtype=jnp.int32)).reshape(-1)
    z = (jnp.stack([me ^ d for d in blocks])[:, None] * cells + jnp.arange(cells, dtype=jnp.int32)).reshape(-1)
    index = (k[:, None] * z[None, :]) % span_total
    phase = index.astype(jnp.float32) * (2.0 * math.pi / span_total)
    tab = jnp.stack([jnp.cos(phase), -jnp.sin(phase)], axis=1) * (1.0 / math.sqrt(span_total))
    return tab.reshape(len(owners), waves, 2, len(blocks) * cells)


def near_terms(ext, cpl, r, row, comps, normal):
    lane = lax.broadcasted_iota(jnp.int32, (8, normal), 1)
    parts = []
    for c in range(comps):
        mid = ext[c, r, pl.ds(row, 8), :]
        up = jnp.where(lane < normal - 1, pltpu.roll(mid, normal - 1, 1), 0.0)
        down = jnp.where(lane > 0, pltpu.roll(mid, 1, 1), 0.0)
        parts.append((ext[c, r, pl.ds(row + 1, 8), :], ext[c, r, pl.ds(row - 1, 8), :], up, down))
    out = []
    for c in range(comps):
        acc = None
        for e in range(comps):
            for d in range(4):
                term = cpl[d, c, e] * parts[e][d]
                acc = term if acc is None else acc + term
        out.append(acc)
    return out


def near_kernel(cpl, state, left, right, near, ext):
    waves, comps, _, rows, normal = state.shape

    def one(k, carry):
        ext[:, :, 8 : 8 + rows, :] = state[k]
        ext[:, :, 7:8, :] = left[k]
        ext[:, :, 8 + rows : 9 + rows, :] = right[k]
        for r in range(2):
            for t in range(rows // 8):
                sums = near_terms(ext, cpl, r, 8 + 8 * t, comps, normal)
                for c in range(comps):
                    near[k, c, r, 8 * t : 8 * t + 8, :] = sums[c]
        return carry

    lax.fori_loop(0, waves, one, 0)


def rotate(re, im, a, b, keep):
    scale = keep / (a * a + b * b)
    return (a * re + b * im) * scale, (a * im - b * re) * scale


def edge_kernel(speed, rhs, near, diag, keep, first):
    waves, comps, _, rows, _ = rhs.shape
    cells = near.shape[3]
    half = rows // 2
    base = pl.program_id(0) * waves

    def one(k, carry):
        for c in range(comps):
            b = speed[base + k, c]
            for lo, at in ((0, 0), (half, cells - half)):
                for t in range(0, half, 8):
                    src, dst = slice(at + t, at + t + 8), slice(lo + t, lo + t + 8)
                    re = rhs[k, c, 0, dst, :] - near[k, c, 0, src, :]
                    im = rhs[k, c, 1, dst, :] - near[k, c, 1, src, :]
                    out = rotate(re, im, diag[c, src, :], b, keep[src, :])
                    first[k, c, 0, dst, :], first[k, c, 1, dst, :] = out
        return carry

    lax.fori_loop(0, waves, one, 0)


def last_kernel(start, cpl, speed, edge_rhs, edge_first, mid_own, mid_far, near, left, right, diag, keep, *rest):
    flow, ext = rest[-2:]
    waves, comps, _, rows, normal = flow.shape
    half = edge_rhs.shape[3] // 2
    base = (start + pl.program_id(0)) * waves

    def one(k, carry):
        ext[:, :, 7:8, :] = left[k]
        ext[:, :, 8 : 8 + half, :] = edge_first[k, :, :, :half, :]
        ext[:, :, 8 + rows - half : 8 + rows, :] = edge_first[k, :, :, half:, :]
        ext[:, :, 8 + rows : 9 + rows, :] = right[k]
        for c in range(comps):
            b = speed[base + k, c]
            for t in range(half, rows - half, 8):
                at = slice(t - half, t - half + 8)
                src = slice(t, t + 8)
                re = mid_own[k, c, 0, at, :] + mid_far[k, c, 0, at, :] - near[k, c, 0, src, :]
                im = mid_own[k, c, 1, at, :] + mid_far[k, c, 1, at, :] - near[k, c, 1, src, :]
                out = rotate(re, im, diag[c, src, :], b, keep[src, :])
                ext[c, 0, 8 + t : 16 + t, :], ext[c, 1, 8 + t : 16 + t, :] = out
        for t in range(0, rows, 8):
            src = slice(t, t + 8)
            sums = [near_terms(ext, cpl, r, 8 + t, comps, normal) for r in range(2)]
            for c in range(comps):
                if t < half or t >= rows - half:
                    lo = t if t < half else t - (rows - 2 * half)
                    rhs = [edge_rhs[k, c, r, lo : lo + 8, :] for r in range(2)]
                else:
                    at = slice(t - half, t - half + 8)
                    rhs = [mid_own[k, c, r, at, :] + mid_far[k, c, r, at, :] for r in range(2)]
                b = speed[base + k, c]
                out = rotate(rhs[0] - sums[0][c], rhs[1] - sums[1][c], diag[c, src, :], b, keep[src, :])
                flow[k, c, 0, src, :], flow[k, c, 1, src, :] = out
        return carry

    lax.fori_loop(0, waves, one, 0)


def by_wave(shape, step, offset=0):
    rest = len(shape) - 1
    return pl.BlockSpec((step,) + tuple(shape[1:]), lambda i: (i + offset,) + (0,) * rest)


def whole(shape):
    return pl.BlockSpec(tuple(shape), lambda i: (0,) * len(shape))


SMEM = pl.BlockSpec(memory_space=pltpu.SMEM)
PARAMS = pltpu.CompilerParams(vmem_limit_bytes=48 * 1024 * 1024)


def cost(flops, moved):
    return pl.CostEstimate(flops=int(flops), bytes_accessed=int(moved), transcendentals=0)


def shards(forcing, initial_state, diagonal, span_speed, coupling, stiffener_mask, face_index, mode_shapes):
    span_count = lax.axis_size("span")
    stream_count = lax.axis_size("stream")
    me = lax.axis_index("span")
    comps, cells, rows, normal = forcing.shape
    waves = initial_state.shape[0]
    span_total = cells * span_count
    half_span = span_count // 2
    modes = face_index.shape[0]
    edge = rows // 4
    table = functools.partial(wave_rows, me=me, waves=waves, cells=cells, span_total=span_total)
    inner = [d for d in (1 << i for i in range(20)) if d < half_span]

    edges = jnp.concatenate([forcing[:, :, :edge], forcing[:, :, rows - edge :]], axis=2)
    middle = forcing[:, :, edge : rows - edge]
    edges_far = swap(edges, "span", half_span)
    blocks, held = [0], middle
    for d in reversed(inner):
        held = jnp.concatenate([held, swap(held, "span", d)], axis=1)
        blocks = blocks + [b ^ d for b in blocks]
    both = jnp.einsum("czxy,dkrz->dkcrxy", held, table([half_span, 0], blocks), precision=HI)
    mid_own = both[1]
    mid_far = swap(both[0], "span", half_span)

    first_cell = lax.axis_index("stream") * rows
    keep = lax.dynamic_slice_in_dim((1 - stiffener_mask).astype(jnp.float32), first_cell, rows, 0)
    diag = lax.dynamic_slice_in_dim(diagonal, first_cell, rows, 1)
    k_mine = me * waves + jnp.arange(waves, dtype=jnp.int32)
    speed = (k_mine.astype(jnp.float32) * (2.0 * math.pi / span_total))[:, None] * span_speed[None, :]
    left0, right0 = halo(initial_state[:, :, :, :1], initial_state[:, :, :, rows - 1 :], "stream")
    step = 2
    grid = (waves // step,)
    state_shape = initial_state.shape
    side_shape = left0.shape
    ext_shape = (comps, 2, rows + 16, normal)
    size = initial_state.size
    near0 = pl.pallas_call(
        near_kernel,
        grid=grid,
        in_specs=[SMEM, by_wave(state_shape, step), by_wave(side_shape, step), by_wave(side_shape, step)],
        out_specs=by_wave(state_shape, step),
        out_shape=jax.ShapeDtypeStruct(state_shape, jnp.float32),
        scratch_shapes=[pltpu.VMEM(ext_shape, jnp.float32)],
        compiler_params=PARAMS,
        cost_estimate=cost(40 * size, 8 * size),
        name="near",
    )(coupling, initial_state, left0, right0)

    pair = jnp.concatenate([edges, edges_far], axis=1)
    owners = [0]
    for d in inner:
        owners = owners + [o ^ d for o in owners]
    part = jnp.einsum("czxy,dkrz->dkcrxy", pair, table(owners, [0, half_span]), precision=HI)
    held_owners = owners
    for d in inner:
        mine = [i for i, o in enumerate(held_owners) if not o & d]
        other = [held_owners.index(held_owners[i] ^ d) for i in mine]
        sent = jnp.stack([part[i] for i in other]) if len(other) > 1 else part[other[0]][None]
        got = swap(sent, "span", d)
        part = jnp.stack([part[i] + got[n] for n, i in enumerate(mine)])
        held_owners = [held_owners[i] for i in mine]
    edge_rhs = part[0]
    edge_shape = edge_rhs.shape
    edge_first = pl.pallas_call(
        edge_kernel,
        grid=grid,
        in_specs=[SMEM, by_wave(edge_shape, step), by_wave(state_shape, step), whole(diag.shape), whole(keep.shape)],
        out_specs=by_wave(edge_shape, step),
        out_shape=jax.ShapeDtypeStruct(edge_shape, jnp.float32),
        compiler_params=PARAMS,
        cost_estimate=cost(10 * size, 8 * size),
        name="edge",
    )(speed, edge_rhs, near0, diag, keep)
    left1, right1 = halo(edge_first[:, :, :, :1], edge_first[:, :, :, 2 * edge - 1 :], "stream")

    flow = pl.pallas_call(
        functools.partial(last_kernel, 0),
        grid=grid,
        in_specs=[SMEM, SMEM]
        + [by_wave(edge_shape, step)] * 2
        + [by_wave(mid_own.shape, step)] * 2
        + [by_wave(state_shape, step)]
        + [by_wave(side_shape, step)] * 2
        + [whole(diag.shape), whole(keep.shape)],
        out_specs=by_wave(state_shape, step),
        out_shape=jax.ShapeDtypeStruct(state_shape, jnp.float32),
        scratch_shapes=[pltpu.VMEM(ext_shape, jnp.float32)],
        compiler_params=PARAMS,
        cost_estimate=cost(50 * size, 16 * size),
        name="last",
    )(coupling, speed, edge_rhs, edge_first, mid_own, mid_far, near0, left1, right1, diag, keep)

    hot = (face_index[:, :, None] == jnp.arange(cells * rows, dtype=jnp.int32)).astype(jnp.float32)
    grid_modes = jnp.einsum("mrf,mfl->mrl", mode_shapes, hot, precision=HI)
    held = grid_modes.reshape(modes * 2, cells, rows)
    blocks = [0]
    for d in [half_span] + inner[::-1]:
        held = jnp.concatenate([held, swap(held, "span", d)], axis=1)
        blocks = blocks + [b ^ d for b in blocks]
    weight = jnp.where(k_mine == 0, 1.0, 2.0).astype(jnp.float32)
    gains = jnp.einsum("mzx,krz->mkrx", held, table([0], blocks)[0], precision=HI) * weight[:, None, None]
    wall = flow[:, comps - 1, :, :, 0]
    total = jnp.sum(gains * wall[None], axis=(1, 2, 3)).reshape(modes, 2)
    for axis, count in (("span", span_count), ("stream", stream_count)):
        d = 1
        while d < count:
            total = total + swap(total, axis, d)
            d *= 2
    faces = face_index.shape[1] * stream_count * span_count
    return flow, total / math.sqrt(faces)


def solution(mesh):
    return jax.shard_map(
        shards,
        mesh=mesh,
        in_specs=(
            P(None, "span", "stream", None),
            P("span", None, None, "stream", None),
            P(),
            P(),
            P(),
            P(),
            P(None, ("stream", "span")),
            P(None, None, ("stream", "span")),
        ),
        out_specs=(P("span", None, None, "stream", None), P()),
        check_vma=False,
    )
```

```python
import functools
import math

import jax
import jax.numpy as jnp
from jax import lax
from jax.experimental import pallas as pl
from jax.experimental.pallas import tpu as pltpu
from jax.sharding import PartitionSpec as P

HI = lax.Precision.HIGHEST


def swap(value, axis, dist):
    count = lax.axis_size(axis)
    return lax.ppermute(value, axis, [(i, i ^ dist) for i in range(count)])


def halo(head, tail, axis):
    ends = lax.axis_size(axis) - 1
    left = lax.ppermute(tail, axis, [(i, i + 1) for i in range(ends)])
    right = lax.ppermute(head, axis, [(i + 1, i) for i in range(ends)])
    return left, right


def gate(value, *after):
    return pl.pallas_call(
        lambda *refs: None,
        in_specs=[pl.BlockSpec(memory_space=pl.ANY)] * (1 + len(after)),
        out_specs=pl.BlockSpec(memory_space=pl.ANY),
        out_shape=jax.ShapeDtypeStruct(value.shape, value.dtype),
        input_output_aliases={0: 0},
        cost_estimate=FREE,
        name="gate",
    )(value, *after)


def split_kernel(start, end, faces, outer, between):
    @pl.when(pl.program_id(0) < pl.num_programs(0) - 1)
    def _():
        outer[:, :4, :] = start[0, :, :4, :]
        outer[:, 4:, :] = end[0, :, 4:, :]
        between[0, :, :4, :] = end[0, :, :4, :]
        between[0, :, 4:, :] = start[0, :, 4:, :]

    @pl.when(pl.program_id(0) == pl.num_programs(0) - 1)
    def _():
        outer[0] = faces[...]


def split(source, faces):
    comps, cells, rows, normal = source.shape
    last = comps - 1

    def spec(tile):
        return pl.BlockSpec((1, cells, 8, normal), lambda c: (jnp.minimum(c, last), 0, tile, 0))

    return pl.pallas_call(
        split_kernel,
        grid=(comps + 1,),
        in_specs=[spec(0), spec(rows // 8 - 1), pl.BlockSpec(faces.shape, lambda c: (0, 0))],
        out_specs=[pl.BlockSpec((cells, 8, normal), lambda c: (c, 0, 0)), spec(0)],
        out_shape=[
            jax.ShapeDtypeStruct((comps * cells + 1, 8, normal), jnp.float32),
            jax.ShapeDtypeStruct((comps, cells, 8, normal), jnp.float32),
        ],
        compiler_params=PARAMS,
        cost_estimate=FREE,
        name="split",
    )(source, source, faces)


def wave_rows(owners, blocks, me, waves, cells, span_total):
    k = (jnp.stack([me ^ d for d in owners])[:, None] * waves + jnp.arange(waves, dtype=jnp.int32)).reshape(-1)
    z = jnp.concatenate([(me ^ d) * cells + start + jnp.arange(size, dtype=jnp.int32) for d, start, size in blocks])
    index = (k[:, None] * z[None, :]) % span_total
    phase = index.astype(jnp.float32) * (2.0 * math.pi / span_total)
    tab = jnp.stack([jnp.cos(phase), -jnp.sin(phase)], axis=1) * (1.0 / math.sqrt(span_total))
    return tab.reshape(len(owners) * waves * 2, z.shape[0])


def halves(value):
    high = value.astype(jnp.bfloat16)
    return high, (value - high.astype(jnp.float32)).astype(jnp.bfloat16)


def table_halves(value):
    high = lax.reduce_precision(value, 8, 7)
    return high.astype(jnp.bfloat16), (value - high).astype(jnp.bfloat16)


def transform_kernel(count, outs_at, sizes, rows, comps, *refs):
    high, low = refs[0], refs[1]
    raws, outs = refs[2 : 2 + count], refs[outs_at:]
    normal = raws[0].shape[-1]
    wide = 2

    @pl.when(pl.program_id(0) < comps)
    def _():
        for x in range(0, rows, wide):
            cols = []
            for j in range(wide):
                cols.append(jnp.concatenate([r[pl.ds(x + j, n, stride=rows), :] for r, n in zip(raws, sizes)], axis=0))
            data = jnp.concatenate(cols, axis=1)
            dh, dl = halves(data)
            dot = functools.partial(jnp.dot, preferred_element_type=jnp.float32)
            val = dot(high[...], dh) + (dot(low[...], dh) + dot(high[...], dl))
            at = 0
            for out in outs:
                lines = out.shape[0] // rows
                for j in range(wide):
                    out[pl.ds(x + j, lines, stride=rows), :] = val[at : at + lines, j * normal : (j + 1) * normal]
                at += lines

    @pl.when(pl.program_id(0) == comps)
    def _():
        for n, raw in enumerate(raws):
            outs[-1][8 * n : 8 * n + 8, :] = raw[:8, :]


def transform(table, raws, lines, after, name, comps, tail=False):
    rows, normal = raws[0].shape[-2:]
    flat = [raw.reshape(-1, normal) for raw in raws]
    sizes = [f.shape[0] // (comps * rows) for f in flat]
    high, low = table_halves(table)
    counts = [comps * n * rows for n in lines]
    if tail:
        counts[-1] += 8 * len(raws)
    first_outs = [pl.BlockSpec((n * rows, normal), lambda c: (jnp.minimum(c, comps - 1), 0)) for n in lines[:-1]]
    outs = pl.pallas_call(
        functools.partial(transform_kernel, len(raws), 2 + len(raws) + len(after), sizes, rows, comps),
        grid=(comps + tail,),
        in_specs=[pl.BlockSpec(table.shape, lambda c: (0, 0))] * 2
        + [pl.BlockSpec((n * rows, normal), lambda c: (c, 0)) for n in sizes]
        + [ANY] * len(after),
        out_specs=first_outs + [pl.BlockSpec((lines[-1] * rows, normal), lambda c: (c, 0))],
        out_shape=[jax.ShapeDtypeStruct((n, normal), jnp.float32) for n in counts],
        compiler_params=PARAMS,
        cost_estimate=FREE,
        name=name,
    )(high, low, *flat, *after)
    return [o if tail and o is outs[-1] else o.reshape(comps, n, rows, normal) for o, n in zip(outs, lines)]


def near_terms(ext, cpl, r, row, comps, normal, wanted):
    lane = lax.broadcasted_iota(jnp.int32, (8, normal), 1)
    parts = []
    for c in range(comps):
        mid = ext[c, r, pl.ds(row, 8), :]
        up = jnp.where(lane < normal - 1, pltpu.roll(mid, normal - 1, 1), 0.0)
        down = jnp.where(lane > 0, pltpu.roll(mid, 1, 1), 0.0)
        parts.append((ext[c, r, pl.ds(row + 1, 8), :], ext[c, r, pl.ds(row - 1, 8), :], up, down))
    out = []
    for c in wanted:
        acc = None
        for e in range(comps):
            for d in range(4):
                term = cpl[d, c, e] * parts[e][d]
                acc = term if acc is None else acc + term
        out.append(acc)
    return out


def near_kernel(cpl, state, left, right, after, near, ext):
    waves, comps, _, rows, normal = state.shape

    def one(k, carry):
        ext[:, :, 8 : 8 + rows, :] = state[k]
        ext[:, :, 7:8, :] = left[k]
        ext[:, :, 8 + rows : 9 + rows, :] = right[k]
        for r in range(2):
            for t in range(rows // 8):
                sums = near_terms(ext, cpl, r, 8 + 8 * t, comps, normal, range(comps))
                for c in range(comps):
                    near[k, c, r, 8 * t : 8 * t + 8, :] = sums[c]
        return carry

    lax.fori_loop(0, waves, one, 0)


def rotate(re, im, a, b, keep):
    scale = keep / (a * a + b * b)
    return (a * re + b * im) * scale, (a * im - b * re) * scale


def edge_kernel(speed, own, far, near_start, near_end, diag, keep, after, first):
    waves, comps, _, _, normal = near_start.shape
    rows = keep.shape[0]
    base = pl.program_id(0) * waves
    low = lax.broadcasted_iota(jnp.int32, (8, normal), 0) < 4

    def one(k, carry):
        for c in range(comps):
            defect = []
            for r in range(2):
                old = jnp.where(low, near_start[k, c, r], near_end[k, c, r])
                defect.append(own[c, 2 * k + r] + far[c, 2 * k + r] - old)
            a = jnp.where(low, diag[c, :8, :], diag[c, rows - 8 :, :])
            out = rotate(*defect, a, speed[base + k, c], jnp.where(low, keep[:8, :], keep[rows - 8 :, :]))
            first[k, c, 0], first[k, c, 1] = out
        return carry

    lax.fori_loop(0, waves, one, 0)


def tile_sums(owns, fars, low, rows, c, at):
    outer, between, *middle = [own[c, at] + far[c, at] for own, far in zip(owns, fars)]
    return [jnp.where(low, outer, between)] + middle + [jnp.where(low, between, outer)]


def last_kernel(pieces, cpl, speed, left, right, diag, keep, near, *rest):
    owns, fars = rest[:pieces], rest[pieces : 2 * pieces]
    flow, ext = rest[2 * pieces :]
    waves, comps, _, rows, normal = flow.shape
    base = pl.program_id(0) * waves
    low = lax.broadcasted_iota(jnp.int32, (8, normal), 0) < 4

    def one(k, carry):
        ext[:, :, 7:8, :] = left[k]
        ext[:, :, 8 + rows : 9 + rows, :] = right[k]
        for c in range(comps):
            b = speed[base + k, c]
            rhs = [tile_sums(owns, fars, low, rows, c, 2 * k + r) for r in range(2)]
            for n in range(rows // 8):
                src = slice(8 * n, 8 * n + 8)
                re, im = (rhs[r][n] - near[k, c, r, src, :] for r in range(2))
                re, im = rotate(re, im, diag[c, src, :], b, keep[src, :])
                ext[c, 0, 8 + 8 * n : 16 + 8 * n, :], ext[c, 1, 8 + 8 * n : 16 + 8 * n, :] = re, im
                flow[k, c, 0, src, :], flow[k, c, 1, src, :] = rhs[0][n], rhs[1][n]
        for n in range(rows // 8):
            src = slice(8 * n, 8 * n + 8)
            sums = [near_terms(ext, cpl, r, 8 + 8 * n, comps, normal, range(comps)) for r in range(2)]
            for c in range(comps):
                re, im = (flow[k, c, r, src, :] - sums[r][c] for r in range(2))
                out = rotate(re, im, diag[c, src, :], speed[base + k, c], keep[src, :])
                flow[k, c, 0, src, :], flow[k, c, 1, src, :] = out
        return carry

    lax.fori_loop(0, waves, one, 0)


def by_wave(shape, step, skip=0):
    rest = len(shape) - 1
    return pl.BlockSpec((step,) + tuple(shape[1:]), lambda i: (i + skip,) + (0,) * rest)


def by_wave2(shape, step, skip=0):
    return pl.BlockSpec((shape[0], 2 * step) + tuple(shape[2:]), lambda i: (0, i + skip, 0, 0))


def whole(shape):
    return pl.BlockSpec(tuple(shape), lambda i: (0,) * len(shape))


SMEM = pl.BlockSpec(memory_space=pltpu.SMEM)
ANY = pl.BlockSpec(memory_space=pl.ANY)
LARGE = pltpu.CompilerParams(vmem_limit_bytes=60 * 1024 * 1024)
PARAMS = pltpu.CompilerParams(vmem_limit_bytes=48 * 1024 * 1024)


BUSY = pl.CostEstimate(flops=0, bytes_accessed=60_000_000, transcendentals=0)
FREE = pl.CostEstimate(flops=0, bytes_accessed=0, transcendentals=0)


def shards(forcing, initial_state, diagonal, span_speed, coupling, stiffener_mask, face_index, mode_shapes):
    span_count = lax.axis_size("span")
    stream_count = lax.axis_size("stream")
    me = lax.axis_index("span")
    comps, cells, rows, normal = forcing.shape
    waves = initial_state.shape[0]
    span_total = cells * span_count
    half_span = span_count // 2
    modes = face_index.shape[0]
    inner = [d for d in (1 << i for i in range(20)) if d < half_span]

    k_mine = me * waves + jnp.arange(waves, dtype=jnp.int32)
    first_cell = lax.axis_index("stream") * rows
    keep = lax.dynamic_slice_in_dim((1 - stiffener_mask).astype(jnp.float32), first_cell, rows, 0)
    diag = lax.dynamic_slice_in_dim(diagonal, first_cell, rows, 1)
    speed = (k_mine.astype(jnp.float32) * (2.0 * math.pi / span_total))[:, None] * span_speed[None, :]
    left0, right0 = halo(initial_state[:, :, :, :1], initial_state[:, :, :, rows - 1 :], "stream")
    step = 2
    grid = (waves // step,)
    state_shape = initial_state.shape
    side_shape = left0.shape
    ext_shape = (comps, 2, rows + 16, normal)
    top, quarter = half_span, half_span // 2
    lower = [d for d in reversed(inner) if d < quarter]
    middle = [forcing[:, :, at : at + 8] for at in range(8, rows - 8, 8)]
    faces = [face_index.astype(jnp.float32), mode_shapes.reshape(2 * modes, -1)]
    faces = jnp.concatenate(faces + [jnp.zeros((8 - 3 * modes, face_index.shape[1]), jnp.float32)], axis=0)
    outer, between = split(forcing, faces)

    def gather(raw, got, hold, first, last):
        late = gate(got, *hold) if hold else got
        sets = [(raw, 0, 0), (late, first, 0)]
        for d in lower:
            more = []
            for value, block, start in sets:
                cuts = 4 if block & first and value.shape[1] == cells and value.ndim == 4 else 1
                size = value.shape[1] // cuts if value.ndim == 4 else cells
                for n in range(cuts):
                    part = value[:, n * size : (n + 1) * size] if cuts > 1 else value
                    more.append((swap(part, "span", d), block ^ d, start + n * size))
            sets = sets + more
        blocks = [(block, start, value.shape[1] if value.ndim == 4 else cells) for value, block, start in sets]
        return [value for value, _, _ in sets], wave_rows([0, last], blocks, me, waves, cells, span_total), [b for b, _, _ in blocks]

    e_got = swap(outer, "span", quarter)
    far_raw = swap(forcing[:, :, 8 : rows - 8], "span", top)
    raws, tab, face_blocks = gather(outer, e_got, [], quarter, top)
    lines = 2 * waves
    e_own, e_out = transform(tab, raws, (lines, lines), [keep, diag, speed], "gathered", comps, True)
    f_got = swap(gate(between, e_got), "span", quarter)
    f_got = swap(gate(between, e_got), "span", quarter)
    e_far = swap(e_out, "span", top)
    cut = comps * lines * 8
    face_sets = jnp.concatenate([e_out[cut:], e_far[cut:]]).reshape(span_count, 8, -1)
    face_blocks = face_blocks + [b ^ top for b in face_blocks]
    e_far = e_far[:cut].reshape(e_own.shape)

    def cross(n, hold):
        raws, tab, _ = gather(middle[n], far_raw[:, :, 8 * n : 8 * n + 8], hold[:1], top, quarter)
        own, out = transform(tab, raws, (lines, lines), hold, "crossing", comps)
        return own, out, swap(out, "span", quarter)

    raws, tab, _ = gather(between, f_got, [e_out], quarter, top)
    f_own, f_out = transform(tab, raws, (lines, lines), [], "gathered", comps)
    f_far = swap(f_out, "span", top)
    c_own, c_out, c_far = cross(0, [f_out])
    d_own, d_out, d_far = cross(1, [c_out])
    near0 = pl.pallas_call(
        near_kernel,
        grid=grid,
        in_specs=[SMEM, by_wave(state_shape, step), by_wave(side_shape, step), by_wave(side_shape, step), ANY],
        out_specs=by_wave(state_shape, step),
        out_shape=jax.ShapeDtypeStruct(state_shape, jnp.float32),
        scratch_shapes=[pltpu.VMEM(ext_shape, jnp.float32)],
        compiler_params=PARAMS,
        cost_estimate=FREE,
        name="near",
    )(coupling, initial_state, left0, right0, d_out)
    owns, fars = [e_own, f_own, c_own, d_own], [e_far, f_far, c_far, d_far]
    pieces = len(owns)

    first_shape = (waves, comps, 2, 8, normal)
    ends = pl.pallas_call(
        edge_kernel,
        grid=(2,),
        in_specs=[SMEM]
        + [by_wave2(e_own.shape, waves // 2)] * 2
        + [pl.BlockSpec((waves // 2,) + first_shape[1:], lambda i, n=n: (i, 0, 0, n, 0)) for n in (0, rows // 8 - 1)]
        + [whole(diag.shape), whole(keep.shape), ANY],
        out_specs=by_wave(first_shape, waves // 2),
        out_shape=jax.ShapeDtypeStruct(first_shape, jnp.float32),
        compiler_params=LARGE,
        cost_estimate=FREE,
        name="edge",
    )(speed, e_own, e_far, near0, near0, diag, keep, c_far)
    left1, right1 = halo(ends[:, :, :, :1], ends[:, :, :, 7:], "stream")

    hot = (face_sets[:, :modes, :, None] == jnp.arange(cells * rows, dtype=jnp.float32)).astype(jnp.float32)
    shapes = face_sets[:, modes : 3 * modes].reshape(span_count, modes, 2, -1)
    held = jnp.einsum("bmrf,bmfl->mrbl", shapes, hot, precision=HI).reshape(2 * modes, span_total, rows)
    tab = wave_rows([0], [(b, 0, cells) for b in face_blocks], me, waves, cells, span_total)
    weight = jnp.where(k_mine == 0, 1.0, 2.0).astype(jnp.float32)
    gains = jnp.einsum("mzx,kz->mkx", held, tab, precision=HI).reshape(2 * modes, waves, 2, rows)
    gains = gains * weight[:, None, None]

    flow = pl.pallas_call(
        functools.partial(last_kernel, pieces),
        grid=grid,
        in_specs=[SMEM, SMEM]
        + [by_wave(side_shape, step)] * 2
        + [whole(diag.shape), whole(keep.shape), by_wave(state_shape, step)]
        + [by_wave2(e_own.shape, step)] * (2 * pieces),
        out_specs=by_wave(state_shape, step),
        out_shape=jax.ShapeDtypeStruct(state_shape, jnp.float32),
        scratch_shapes=[pltpu.VMEM(ext_shape, jnp.float32)],
        compiler_params=LARGE,
        cost_estimate=FREE,
        name="last",
    )(coupling, speed, left1, right1, diag, keep, near0, *owns, *fars)

    wall = flow[:, comps - 1, :, :, 0]
    total = jnp.sum(gains * wall[None], axis=(1, 2, 3)).reshape(modes, 2)
    for axis, count in (("span", span_count), ("stream", stream_count)):
        d = 1
        while d < count:
            total = total + swap(total, axis, d)
            d *= 2
    faces = face_index.shape[1] * stream_count * span_count
    return flow, total / math.sqrt(faces)


def solution(mesh):
    return jax.shard_map(
        shards,
        mesh=mesh,
        in_specs=(
            P(None, "span", "stream", None),
            P("span", None, None, "stream", None),
            P(),
            P(),
            P(),
            P(),
            P(None, ("stream", "span")),
            P(None, None, ("stream", "span")),
        ),
        out_specs=(P("span", None, None, "stream", None), P()),
        check_vma=False,
    )
```

```python
import functools
import math

import jax
import jax.numpy as jnp
from jax import lax
from jax.experimental import pallas as pl
from jax.experimental.pallas import tpu as pltpu
from jax.sharding import PartitionSpec as P

HI = lax.Precision.HIGHEST


def swap(value, axis, dist):
    count = lax.axis_size(axis)
    return lax.ppermute(value, axis, [(i, i ^ dist) for i in range(count)])


def halo(head, tail, axis):
    ends = lax.axis_size(axis) - 1
    left = lax.ppermute(tail, axis, [(i, i + 1) for i in range(ends)])
    right = lax.ppermute(head, axis, [(i + 1, i) for i in range(ends)])
    return left, right


def gate(value, *after):
    return pl.pallas_call(
        lambda *refs: None,
        in_specs=[pl.BlockSpec(memory_space=pl.ANY)] * (1 + len(after)),
        out_specs=pl.BlockSpec(memory_space=pl.ANY),
        out_shape=jax.ShapeDtypeStruct(value.shape, value.dtype),
        input_output_aliases={0: 0},
        cost_estimate=FREE,
        name="gate",
    )(value, *after)


def split_kernel(start, end, faces, after, outer, between):
    @pl.when(pl.program_id(0) < pl.num_programs(0) - 1)
    def _():
        outer[:, :4, :] = start[0, :, :4, :]
        outer[:, 4:, :] = end[0, :, 4:, :]
        between[0, :, :4, :] = end[0, :, :4, :]
        between[0, :, 4:, :] = start[0, :, 4:, :]

    @pl.when(pl.program_id(0) == pl.num_programs(0) - 1)
    def _():
        outer[0] = faces[...]


def split(source, faces, after):
    comps, cells, rows, normal = source.shape
    last = comps - 1

    def spec(tile):
        return pl.BlockSpec((1, cells, 8, normal), lambda c: (jnp.minimum(c, last), 0, tile, 0))

    return pl.pallas_call(
        split_kernel,
        grid=(comps + 1,),
        in_specs=[spec(0), spec(rows // 8 - 1), pl.BlockSpec(faces.shape, lambda c: (0, 0)), ANY],
        out_specs=[pl.BlockSpec((cells, 8, normal), lambda c: (c, 0, 0)), spec(0)],
        out_shape=[
            jax.ShapeDtypeStruct((comps * cells + 1, 8, normal), jnp.float32),
            jax.ShapeDtypeStruct((comps, cells, 8, normal), jnp.float32),
        ],
        compiler_params=PARAMS,
        cost_estimate=FREE,
        name="split",
    )(source, source, faces, after)


def wave_rows(owners, blocks, me, waves, cells, span_total):
    k = (jnp.stack([me ^ d for d in owners])[:, None] * waves + jnp.arange(waves, dtype=jnp.int32)).reshape(-1)
    z = jnp.concatenate([(me ^ d) * cells + start + jnp.arange(size, dtype=jnp.int32) for d, start, size in blocks])
    index = (k[:, None] * z[None, :]) % span_total
    phase = index.astype(jnp.float32) * (2.0 * math.pi / span_total)
    tab = jnp.stack([jnp.cos(phase), -jnp.sin(phase)], axis=1) * (1.0 / math.sqrt(span_total))
    return tab.reshape(len(owners) * waves * 2, z.shape[0])


def halves(value):
    high = value.astype(jnp.bfloat16)
    return high, (value - high.astype(jnp.float32)).astype(jnp.bfloat16)


def table_halves(value):
    high = lax.reduce_precision(value, 8, 7)
    return high.astype(jnp.bfloat16), (value - high).astype(jnp.bfloat16)


def transform_kernel(count, outs_at, sizes, rows, comps, *refs):
    high, low = refs[0], refs[1]
    raws, outs = refs[2 : 2 + count], refs[outs_at:]
    normal = raws[0].shape[-1]
    wide = 2

    @pl.when(pl.program_id(0) < comps)
    def _():
        for x in range(0, rows, wide):
            cols = []
            for j in range(wide):
                cols.append(jnp.concatenate([r[pl.ds(x + j, n, stride=rows), :] for r, n in zip(raws, sizes)], axis=0))
            data = jnp.concatenate(cols, axis=1)
            dh, dl = halves(data)
            dot = functools.partial(jnp.dot, preferred_element_type=jnp.float32)
            val = dot(high[...], dh) + (dot(low[...], dh) + dot(high[...], dl))
            at = 0
            for out in outs:
                lines = out.shape[0] // rows
                for j in range(wide):
                    out[pl.ds(x + j, lines, stride=rows), :] = val[at : at + lines, j * normal : (j + 1) * normal]
                at += lines

    @pl.when(pl.program_id(0) == comps)
    def _():
        for n, raw in enumerate(raws):
            outs[-1][8 * n : 8 * n + 8, :] = raw[:8, :]


def transform(table, raws, lines, after, name, comps, tail=False):
    rows, normal = raws[0].shape[-2:]
    flat = [raw.reshape(-1, normal) for raw in raws]
    sizes = [f.shape[0] // (comps * rows) for f in flat]
    high, low = table_halves(table)
    counts = [comps * n * rows for n in lines]
    if tail:
        counts[-1] += 8 * len(raws)
    first_outs = [pl.BlockSpec((n * rows, normal), lambda c: (jnp.minimum(c, comps - 1), 0)) for n in lines[:-1]]
    outs = pl.pallas_call(
        functools.partial(transform_kernel, len(raws), 2 + len(raws) + len(after), sizes, rows, comps),
        grid=(comps + tail,),
        in_specs=[pl.BlockSpec(table.shape, lambda c: (0, 0))] * 2
        + [pl.BlockSpec((n * rows, normal), lambda c: (c, 0)) for n in sizes]
        + [ANY] * len(after),
        out_specs=first_outs + [pl.BlockSpec((lines[-1] * rows, normal), lambda c: (c, 0))],
        out_shape=[jax.ShapeDtypeStruct((n, normal), jnp.float32) for n in counts],
        compiler_params=PARAMS,
        cost_estimate=FREE,
        name=name,
    )(high, low, *flat, *after)
    return [o if tail and o is outs[-1] else o.reshape(comps, n, rows, normal) for o, n in zip(outs, lines)]


def near_terms(ext, cpl, r, row, comps, normal, wanted):
    lane = lax.broadcasted_iota(jnp.int32, (8, normal), 1)
    parts = []
    for c in range(comps):
        mid = ext[c, r, pl.ds(row, 8), :]
        up = jnp.where(lane < normal - 1, pltpu.roll(mid, normal - 1, 1), 0.0)
        down = jnp.where(lane > 0, pltpu.roll(mid, 1, 1), 0.0)
        parts.append((ext[c, r, pl.ds(row + 1, 8), :], ext[c, r, pl.ds(row - 1, 8), :], up, down))
    out = []
    for c in wanted:
        acc = None
        for e in range(comps):
            for d in range(4):
                term = cpl[d, c, e] * parts[e][d]
                acc = term if acc is None else acc + term
        out.append(acc)
    return out


def near_kernel(cpl, state, left, right, after, near, ext):
    waves, comps, _, rows, normal = state.shape

    def one(k, carry):
        ext[:, :, 8 : 8 + rows, :] = state[k]
        ext[:, :, 7:8, :] = left[k]
        ext[:, :, 8 + rows : 9 + rows, :] = right[k]
        for r in range(2):
            for t in range(rows // 8):
                sums = near_terms(ext, cpl, r, 8 + 8 * t, comps, normal, range(comps))
                for c in range(comps):
                    near[k, c, r, 8 * t : 8 * t + 8, :] = sums[c]
        return carry

    lax.fori_loop(0, waves, one, 0)


def rotate(re, im, a, b, keep):
    scale = keep / (a * a + b * b)
    return (a * re + b * im) * scale, (a * im - b * re) * scale


def edge_kernel(speed, own, far, near_start, near_end, diag, keep, after, first):
    waves, comps, _, _, normal = near_start.shape
    rows = keep.shape[0]
    base = pl.program_id(0) * waves
    low = lax.broadcasted_iota(jnp.int32, (8, normal), 0) < 4

    def one(k, carry):
        for c in range(comps):
            defect = []
            for r in range(2):
                old = jnp.where(low, near_start[k, c, r], near_end[k, c, r])
                defect.append(own[c, 2 * k + r] + far[c, 2 * k + r] - old)
            a = jnp.where(low, diag[c, :8, :], diag[c, rows - 8 :, :])
            out = rotate(*defect, a, speed[base + k, c], jnp.where(low, keep[:8, :], keep[rows - 8 :, :]))
            first[k, c, 0], first[k, c, 1] = out
        return carry

    lax.fori_loop(0, waves, one, 0)


def tile_sums(owns, fars, low, rows, c, at):
    outer, between, *middle = [own[c, at] + far[c, at] for own, far in zip(owns, fars)]
    return [jnp.where(low, outer, between)] + middle + [jnp.where(low, between, outer)]


def last_kernel(pieces, cpl, speed, left, right, diag, keep, near, *rest):
    owns, fars = rest[:pieces], rest[pieces : 2 * pieces]
    flow, ext = rest[2 * pieces :]
    waves, comps, _, rows, normal = flow.shape
    base = pl.program_id(0) * waves
    low = lax.broadcasted_iota(jnp.int32, (8, normal), 0) < 4

    def one(k, carry):
        ext[:, :, 7:8, :] = left[k]
        ext[:, :, 8 + rows : 9 + rows, :] = right[k]
        for c in range(comps):
            b = speed[base + k, c]
            rhs = [tile_sums(owns, fars, low, rows, c, 2 * k + r) for r in range(2)]
            for n in range(rows // 8):
                src = slice(8 * n, 8 * n + 8)
                re, im = (rhs[r][n] - near[k, c, r, src, :] for r in range(2))
                re, im = rotate(re, im, diag[c, src, :], b, keep[src, :])
                ext[c, 0, 8 + 8 * n : 16 + 8 * n, :], ext[c, 1, 8 + 8 * n : 16 + 8 * n, :] = re, im
                flow[k, c, 0, src, :], flow[k, c, 1, src, :] = rhs[0][n], rhs[1][n]
        for n in range(rows // 8):
            src = slice(8 * n, 8 * n + 8)
            sums = [near_terms(ext, cpl, r, 8 + 8 * n, comps, normal, range(comps)) for r in range(2)]
            for c in range(comps):
                re, im = (flow[k, c, r, src, :] - sums[r][c] for r in range(2))
                out = rotate(re, im, diag[c, src, :], speed[base + k, c], keep[src, :])
                flow[k, c, 0, src, :], flow[k, c, 1, src, :] = out
        return carry

    lax.fori_loop(0, waves, one, 0)


def by_wave(shape, step, skip=0):
    rest = len(shape) - 1
    return pl.BlockSpec((step,) + tuple(shape[1:]), lambda i: (i + skip,) + (0,) * rest)


def by_wave2(shape, step, skip=0):
    return pl.BlockSpec((shape[0], 2 * step) + tuple(shape[2:]), lambda i: (0, i + skip, 0, 0))


def whole(shape):
    return pl.BlockSpec(tuple(shape), lambda i: (0,) * len(shape))


SMEM = pl.BlockSpec(memory_space=pltpu.SMEM)
ANY = pl.BlockSpec(memory_space=pl.ANY)
LARGE = pltpu.CompilerParams(vmem_limit_bytes=60 * 1024 * 1024)
PARAMS = pltpu.CompilerParams(vmem_limit_bytes=48 * 1024 * 1024)


FREE = pl.CostEstimate(flops=0, bytes_accessed=0, transcendentals=0)


def shards(forcing, initial_state, diagonal, span_speed, coupling, stiffener_mask, face_index, mode_shapes):
    span_count = lax.axis_size("span")
    stream_count = lax.axis_size("stream")
    me = lax.axis_index("span")
    comps, cells, rows, normal = forcing.shape
    waves = initial_state.shape[0]
    span_total = cells * span_count
    half_span = span_count // 2
    modes = face_index.shape[0]
    inner = [d for d in (1 << i for i in range(20)) if d < half_span]

    k_mine = me * waves + jnp.arange(waves, dtype=jnp.int32)
    first_cell = lax.axis_index("stream") * rows
    keep = lax.dynamic_slice_in_dim((1 - stiffener_mask).astype(jnp.float32), first_cell, rows, 0)
    diag = lax.dynamic_slice_in_dim(diagonal, first_cell, rows, 1)
    speed = (k_mine.astype(jnp.float32) * (2.0 * math.pi / span_total))[:, None] * span_speed[None, :]
    left0, right0 = halo(initial_state[:, :, :, :1], initial_state[:, :, :, rows - 1 :], "stream")
    step = 4
    grid = (waves // step,)
    state_shape = initial_state.shape
    side_shape = left0.shape
    ext_shape = (comps, 2, rows + 16, normal)
    top, quarter = half_span, half_span // 2
    lower = [d for d in reversed(inner) if d < quarter]
    middle = [forcing[:, :, at : at + 8] for at in range(8, rows - 8, 8)]
    faces = [face_index.astype(jnp.float32), mode_shapes.reshape(2 * modes, -1)]
    faces = jnp.concatenate(faces + [jnp.zeros((8 - 3 * modes, face_index.shape[1]), jnp.float32)], axis=0)
    inner_rows = forcing[:, :, 8 : rows - 8]
    far_raw = swap(inner_rows, "span", half_span)
    outer, between = split(forcing, faces, inner_rows)

    def gather(raw, got, hold, first, last):
        late = gate(got, *hold) if hold else got
        sets = [(raw, 0, 0), (late, first, 0)]
        for d in lower:
            more = []
            for value, block, start in sets:
                cuts = 4 if block & first and value.shape[1] == cells and value.ndim == 4 else 1
                size = value.shape[1] // cuts if value.ndim == 4 else cells
                for n in range(cuts):
                    part = value[:, n * size : (n + 1) * size] if cuts > 1 else value
                    more.append((swap(part, "span", d), block ^ d, start + n * size))
            sets = sets + more
        blocks = [(block, start, value.shape[1] if value.ndim == 4 else cells) for value, block, start in sets]
        return [value for value, _, _ in sets], wave_rows([0, last], blocks, me, waves, cells, span_total), [b for b, _, _ in blocks]

    e_got = swap(outer, "span", quarter)
    raws, tab, face_blocks = gather(outer, e_got, [], quarter, top)
    lines = 2 * waves
    e_own, e_out = transform(tab, raws, (lines, lines), [keep, diag, speed, left0, right0], "gathered", comps, True)
    f_got = swap(gate(between, e_got), "span", quarter)
    e_far = swap(e_out, "span", top)
    cut = comps * lines * 8
    face_sets = jnp.concatenate([e_out[cut:], e_far[cut:]]).reshape(span_count, 8, -1)
    face_blocks = face_blocks + [b ^ top for b in face_blocks]
    e_far = e_far[:cut].reshape(e_own.shape)

    def cross(n, hold):
        raws, tab, _ = gather(middle[n], far_raw[:, :, 8 * n : 8 * n + 8], hold[:1], top, quarter)
        own, out = transform(tab, raws, (lines, lines), hold, "crossing", comps)
        return own, out, swap(out, "span", quarter)

    raws, tab, _ = gather(between, f_got, [e_out], quarter, top)
    f_own, f_out = transform(tab, raws, (lines, lines), [], "gathered", comps)
    f_far = swap(f_out, "span", top)
    c_own, c_out, c_far = cross(0, [f_out])
    d_own, d_out, d_far = cross(1, [c_out])
    near0 = pl.pallas_call(
        near_kernel,
        grid=grid,
        in_specs=[SMEM, by_wave(state_shape, step), by_wave(side_shape, step), by_wave(side_shape, step), ANY],
        out_specs=by_wave(state_shape, step),
        out_shape=jax.ShapeDtypeStruct(state_shape, jnp.float32),
        scratch_shapes=[pltpu.VMEM(ext_shape, jnp.float32)],
        compiler_params=PARAMS,
        cost_estimate=FREE,
        name="near",
    )(coupling, initial_state, left0, right0, d_out)
    owns, fars = [e_own, f_own, c_own, d_own], [e_far, f_far, c_far, d_far]
    pieces = len(owns)

    first_shape = (waves, comps, 2, 8, normal)
    ends = pl.pallas_call(
        edge_kernel,
        grid=(2,),
        in_specs=[SMEM]
        + [by_wave2(e_own.shape, waves // 2)] * 2
        + [pl.BlockSpec((waves // 2,) + first_shape[1:], lambda i, n=n: (i, 0, 0, n, 0)) for n in (0, rows // 8 - 1)]
        + [whole(diag.shape), whole(keep.shape), ANY],
        out_specs=by_wave(first_shape, waves // 2),
        out_shape=jax.ShapeDtypeStruct(first_shape, jnp.float32),
        compiler_params=LARGE,
        cost_estimate=FREE,
        name="edge",
    )(speed, e_own, e_far, near0, near0, diag, keep, c_far)
    left1, right1 = halo(ends[:, :, :, :1], ends[:, :, :, 7:], "stream")

    hot = (face_sets[:, :modes, :, None] == jnp.arange(cells * rows, dtype=jnp.float32)).astype(jnp.float32)
    shapes = face_sets[:, modes : 3 * modes].reshape(span_count, modes, 2, -1)
    held = jnp.einsum("bmrf,bmfl->mrbl", shapes, hot, precision=HI).reshape(2 * modes, span_total, rows)
    tab = wave_rows([0], [(b, 0, cells) for b in face_blocks], me, waves, cells, span_total)
    weight = jnp.where(k_mine == 0, 1.0, 2.0).astype(jnp.float32)
    gains = jnp.einsum("mzx,kz->mkx", held, tab, precision=HI).reshape(2 * modes, waves, 2, rows)
    gains = gains * weight[:, None, None]

    step = 4
    grid = (waves // step,)
    flow = pl.pallas_call(
        functools.partial(last_kernel, pieces),
        grid=grid,
        in_specs=[SMEM, SMEM]
        + [by_wave(side_shape, step)] * 2
        + [whole(diag.shape), whole(keep.shape), by_wave(state_shape, step)]
        + [by_wave2(e_own.shape, step)] * (2 * pieces),
        out_specs=by_wave(state_shape, step),
        out_shape=jax.ShapeDtypeStruct(state_shape, jnp.float32),
        scratch_shapes=[pltpu.VMEM(ext_shape, jnp.float32)],
        compiler_params=LARGE,
        cost_estimate=FREE,
        name="last",
    )(coupling, speed, left1, right1, diag, keep, near0, *owns, *fars)

    wall = flow[:, comps - 1, :, :, 0]
    total = jnp.sum(gains * wall[None], axis=(1, 2, 3)).reshape(modes, 2)
    for axis, count in (("span", span_count), ("stream", stream_count)):
        d = 1
        while d < count:
            total = total + swap(total, axis, d)
            d *= 2
    faces = face_index.shape[1] * stream_count * span_count
    return flow, total / math.sqrt(faces)


def solution(mesh):
    return jax.shard_map(
        shards,
        mesh=mesh,
        in_specs=(
            P(None, "span", "stream", None),
            P("span", None, None, "stream", None),
            P(),
            P(),
            P(),
            P(),
            P(None, ("stream", "span")),
            P(None, None, ("stream", "span")),
        ),
        out_specs=(P("span", None, None, "stream", None), P()),
        check_vma=False,
    )
```

```python
import functools
import math

import jax
import jax.numpy as jnp
from jax import lax
from jax.experimental import pallas as pl
from jax.experimental.pallas import tpu as pltpu
from jax.sharding import PartitionSpec as P

HI = lax.Precision.HIGHEST


def swap(value, axis, dist):
    count = lax.axis_size(axis)
    return lax.ppermute(value, axis, [(i, i ^ dist) for i in range(count)])


def halo(head, tail, axis):
    ends = lax.axis_size(axis) - 1
    left = lax.ppermute(tail, axis, [(i, i + 1) for i in range(ends)])
    right = lax.ppermute(head, axis, [(i + 1, i) for i in range(ends)])
    return left, right


def gate(value, *after):
    return pl.pallas_call(
        lambda *refs: None,
        in_specs=[pl.BlockSpec(memory_space=pl.ANY)] * (1 + len(after)),
        out_specs=pl.BlockSpec(memory_space=pl.ANY),
        out_shape=jax.ShapeDtypeStruct(value.shape, value.dtype),
        input_output_aliases={0: 0},
        cost_estimate=FREE,
        name="gate",
    )(value, *after)


def split_kernel(start, end, faces, after, outer, between):
    @pl.when(pl.program_id(0) < pl.num_programs(0) - 1)
    def _():
        outer[:, :4, :] = start[0, :, :4, :]
        outer[:, 4:, :] = end[0, :, 4:, :]
        between[0, :, :4, :] = end[0, :, :4, :]
        between[0, :, 4:, :] = start[0, :, 4:, :]

    @pl.when(pl.program_id(0) == pl.num_programs(0) - 1)
    def _():
        outer[0] = faces[...]


def split(source, faces, after):
    comps, cells, rows, normal = source.shape
    last = comps - 1

    def spec(tile):
        return pl.BlockSpec((1, cells, 8, normal), lambda c: (jnp.minimum(c, last), 0, tile, 0))

    return pl.pallas_call(
        split_kernel,
        grid=(comps + 1,),
        in_specs=[spec(0), spec(rows // 8 - 1), pl.BlockSpec(faces.shape, lambda c: (0, 0)), ANY],
        out_specs=[pl.BlockSpec((cells, 8, normal), lambda c: (c, 0, 0)), spec(0)],
        out_shape=[
            jax.ShapeDtypeStruct((comps * cells + 1, 8, normal), jnp.float32),
            jax.ShapeDtypeStruct((comps, cells, 8, normal), jnp.float32),
        ],
        compiler_params=PARAMS,
        cost_estimate=FREE,
        name="split",
    )(source, source, faces, after)


def wave_rows(owners, blocks, me, waves, cells, span_total):
    k = (jnp.stack([me ^ d for d in owners])[:, None] * waves + jnp.arange(waves, dtype=jnp.int32)).reshape(-1)
    z = jnp.concatenate([(me ^ d) * cells + start + jnp.arange(size, dtype=jnp.int32) for d, start, size in blocks])
    index = (k[:, None] * z[None, :]) % span_total
    phase = index.astype(jnp.float32) * (2.0 * math.pi / span_total)
    tab = jnp.stack([jnp.cos(phase), -jnp.sin(phase)], axis=1) * (1.0 / math.sqrt(span_total))
    return tab.reshape(len(owners) * waves * 2, z.shape[0])


def halves(value):
    high = value.astype(jnp.bfloat16)
    return high, (value - high.astype(jnp.float32)).astype(jnp.bfloat16)


def table_halves(value):
    high = lax.reduce_precision(value, 8, 7)
    return high.astype(jnp.bfloat16), (value - high).astype(jnp.bfloat16)


def transform_kernel(count, outs_at, sizes, rows, comps, *refs):
    high, low = refs[0], refs[1]
    raws, outs = refs[2 : 2 + count], refs[outs_at:]
    normal = raws[0].shape[-1]
    wide = 2

    @pl.when(pl.program_id(0) < comps)
    def _():
        for x in range(0, rows, wide):
            cols = []
            for j in range(wide):
                cols.append(jnp.concatenate([r[pl.ds(x + j, n, stride=rows), :] for r, n in zip(raws, sizes)], axis=0))
            data = jnp.concatenate(cols, axis=1)
            dh, dl = halves(data)
            dot = functools.partial(jnp.dot, preferred_element_type=jnp.float32)
            val = dot(high[...], dh) + (dot(low[...], dh) + dot(high[...], dl))
            at = 0
            for out in outs:
                lines = out.shape[0] // rows
                for j in range(wide):
                    out[pl.ds(x + j, lines, stride=rows), :] = val[at : at + lines, j * normal : (j + 1) * normal]
                at += lines

    @pl.when(pl.program_id(0) == comps)
    def _():
        for n, raw in enumerate(raws):
            outs[-1][8 * n : 8 * n + 8, :] = raw[:8, :]


def transform(table, raws, lines, after, name, comps, tail=False):
    rows, normal = raws[0].shape[-2:]
    flat = [raw.reshape(-1, normal) for raw in raws]
    sizes = [f.shape[0] // (comps * rows) for f in flat]
    high, low = table_halves(table)
    counts = [comps * n * rows for n in lines]
    if tail:
        counts[-1] += 8 * len(raws)
    first_outs = [pl.BlockSpec((n * rows, normal), lambda c: (jnp.minimum(c, comps - 1), 0)) for n in lines[:-1]]
    outs = pl.pallas_call(
        functools.partial(transform_kernel, len(raws), 2 + len(raws) + len(after), sizes, rows, comps),
        grid=(comps + tail,),
        in_specs=[pl.BlockSpec(table.shape, lambda c: (0, 0))] * 2
        + [pl.BlockSpec((n * rows, normal), lambda c: (c, 0)) for n in sizes]
        + [ANY] * len(after),
        out_specs=first_outs + [pl.BlockSpec((lines[-1] * rows, normal), lambda c: (c, 0))],
        out_shape=[jax.ShapeDtypeStruct((n, normal), jnp.float32) for n in counts],
        compiler_params=PARAMS,
        cost_estimate=FREE,
        name=name,
    )(high, low, *flat, *after)
    return [o if tail and o is outs[-1] else o.reshape(comps, n, rows, normal) for o, n in zip(outs, lines)]


def near_terms(ext, cpl, r, row, comps, normal, wanted):
    lane = lax.broadcasted_iota(jnp.int32, (8, normal), 1)
    parts = []
    for c in range(comps):
        mid = ext[c, r, pl.ds(row, 8), :]
        up = jnp.where(lane < normal - 1, pltpu.roll(mid, normal - 1, 1), 0.0)
        down = jnp.where(lane > 0, pltpu.roll(mid, 1, 1), 0.0)
        parts.append((ext[c, r, pl.ds(row + 1, 8), :], ext[c, r, pl.ds(row - 1, 8), :], up, down))
    out = []
    for c in wanted:
        acc = None
        for e in range(comps):
            for d in range(4):
                term = cpl[d, c, e] * parts[e][d]
                acc = term if acc is None else acc + term
        out.append(acc)
    return out


def near_kernel(cpl, state, left, right, after, near, ext):
    waves, comps, _, rows, normal = state.shape

    def one(k, carry):
        ext[:, :, 8 : 8 + rows, :] = state[k]
        ext[:, :, 7:8, :] = left[k]
        ext[:, :, 8 + rows : 9 + rows, :] = right[k]
        for r in range(2):
            for t in range(rows // 8):
                sums = near_terms(ext, cpl, r, 8 + 8 * t, comps, normal, range(comps))
                for c in range(comps):
                    near[k, c, r, 8 * t : 8 * t + 8, :] = sums[c]
        return carry

    lax.fori_loop(0, waves, one, 0)


def rotate(re, im, a, b, keep):
    scale = keep / (a * a + b * b)
    return (a * re + b * im) * scale, (a * im - b * re) * scale


def edge_kernel(speed, own, far, near_start, near_end, diag, keep, after, first):
    waves, comps, _, _, normal = near_start.shape
    rows = keep.shape[0]
    base = pl.program_id(0) * waves
    low = lax.broadcasted_iota(jnp.int32, (8, normal), 0) < 4

    def one(k, carry):
        for c in range(comps):
            defect = []
            for r in range(2):
                old = jnp.where(low, near_start[k, c, r], near_end[k, c, r])
                defect.append(own[c, 2 * k + r] + far[c, 2 * k + r] - old)
            a = jnp.where(low, diag[c, :8, :], diag[c, rows - 8 :, :])
            out = rotate(*defect, a, speed[base + k, c], jnp.where(low, keep[:8, :], keep[rows - 8 :, :]))
            first[k, c, 0], first[k, c, 1] = out
        return carry

    lax.fori_loop(0, waves, one, 0)


def tile_sums(owns, fars, low, rows, c, at):
    outer, between, middle = [own[c, at] + far[c, at] for own, far in zip(owns, fars)]
    middle = [middle[t : t + 8] for t in range(0, rows - 16, 8)]
    return [jnp.where(low, outer, between)] + middle + [jnp.where(low, between, outer)]


def last_kernel(pieces, cpl, speed, left, right, diag, keep, near, *rest):
    owns, fars = rest[:pieces], rest[pieces : 2 * pieces]
    flow, ext = rest[2 * pieces :]
    waves, comps, _, rows, normal = flow.shape
    base = pl.program_id(0) * waves
    low = lax.broadcasted_iota(jnp.int32, (8, normal), 0) < 4

    def one(k, carry):
        ext[:, :, 7:8, :] = left[k]
        ext[:, :, 8 + rows : 9 + rows, :] = right[k]
        for c in range(comps):
            b = speed[base + k, c]
            rhs = [tile_sums(owns, fars, low, rows, c, 2 * k + r) for r in range(2)]
            for n in range(rows // 8):
                src = slice(8 * n, 8 * n + 8)
                re, im = (rhs[r][n] - near[k, c, r, src, :] for r in range(2))
                re, im = rotate(re, im, diag[c, src, :], b, keep[src, :])
                ext[c, 0, 8 + 8 * n : 16 + 8 * n, :], ext[c, 1, 8 + 8 * n : 16 + 8 * n, :] = re, im
                flow[k, c, 0, src, :], flow[k, c, 1, src, :] = rhs[0][n], rhs[1][n]
        for n in range(rows // 8):
            src = slice(8 * n, 8 * n + 8)
            sums = [near_terms(ext, cpl, r, 8 + 8 * n, comps, normal, range(comps)) for r in range(2)]
            for c in range(comps):
                re, im = (flow[k, c, r, src, :] - sums[r][c] for r in range(2))
                out = rotate(re, im, diag[c, src, :], speed[base + k, c], keep[src, :])
                flow[k, c, 0, src, :], flow[k, c, 1, src, :] = out
        return carry

    lax.fori_loop(0, waves, one, 0)


def by_wave(shape, step, skip=0):
    rest = len(shape) - 1
    return pl.BlockSpec((step,) + tuple(shape[1:]), lambda i: (i + skip,) + (0,) * rest)


def by_wave2(shape, step, skip=0):
    return pl.BlockSpec((shape[0], 2 * step) + tuple(shape[2:]), lambda i: (0, i + skip, 0, 0))


def whole(shape):
    return pl.BlockSpec(tuple(shape), lambda i: (0,) * len(shape))


SMEM = pl.BlockSpec(memory_space=pltpu.SMEM)
ANY = pl.BlockSpec(memory_space=pl.ANY)
LARGE = pltpu.CompilerParams(vmem_limit_bytes=60 * 1024 * 1024)
PARAMS = pltpu.CompilerParams(vmem_limit_bytes=48 * 1024 * 1024)


FREE = pl.CostEstimate(flops=0, bytes_accessed=0, transcendentals=0)


def shards(forcing, initial_state, diagonal, span_speed, coupling, stiffener_mask, face_index, mode_shapes):
    span_count = lax.axis_size("span")
    stream_count = lax.axis_size("stream")
    me = lax.axis_index("span")
    comps, cells, rows, normal = forcing.shape
    waves = initial_state.shape[0]
    span_total = cells * span_count
    half_span = span_count // 2
    modes = face_index.shape[0]
    inner = [d for d in (1 << i for i in range(20)) if d < half_span]

    k_mine = me * waves + jnp.arange(waves, dtype=jnp.int32)
    first_cell = lax.axis_index("stream") * rows
    keep = lax.dynamic_slice_in_dim((1 - stiffener_mask).astype(jnp.float32), first_cell, rows, 0)
    diag = lax.dynamic_slice_in_dim(diagonal, first_cell, rows, 1)
    speed = (k_mine.astype(jnp.float32) * (2.0 * math.pi / span_total))[:, None] * span_speed[None, :]
    left0, right0 = halo(initial_state[:, :, :, :1], initial_state[:, :, :, rows - 1 :], "stream")
    step = 4
    grid = (waves // step,)
    state_shape = initial_state.shape
    side_shape = left0.shape
    ext_shape = (comps, 2, rows + 16, normal)
    top, quarter = half_span, half_span // 2
    lower = [d for d in reversed(inner) if d < quarter]
    faces = [face_index.astype(jnp.float32), mode_shapes.reshape(2 * modes, -1)]
    faces = jnp.concatenate(faces + [jnp.zeros((8 - 3 * modes, face_index.shape[1]), jnp.float32)], axis=0)
    inner_rows = forcing[:, :, 8 : rows - 8]
    far_raw = swap(inner_rows, "span", half_span)
    outer, between = split(forcing, faces, inner_rows)

    def gather(raw, got, hold, first, last):
        late = gate(got, *hold) if hold else got
        sets = [(raw, 0, 0), (late, first, 0)]
        for d in lower:
            more = []
            for value, block, start in sets:
                cuts = 4 if block & first and value.shape[1] == cells and value.ndim == 4 else 1
                size = value.shape[1] // cuts if value.ndim == 4 else cells
                for n in range(cuts):
                    part = value[:, n * size : (n + 1) * size] if cuts > 1 else value
                    more.append((swap(part, "span", d), block ^ d, start + n * size))
            sets = sets + more
        blocks = [(block, start, value.shape[1] if value.ndim == 4 else cells) for value, block, start in sets]
        return [value for value, _, _ in sets], wave_rows([0, last], blocks, me, waves, cells, span_total), [b for b, _, _ in blocks]

    e_got = swap(outer, "span", quarter)
    raws, tab, face_blocks = gather(outer, e_got, [], quarter, top)
    lines = 2 * waves
    e_own, e_out = transform(tab, raws, (lines, lines), [keep, diag, speed, left0, right0], "gathered", comps, True)
    f_got = swap(gate(between, e_got), "span", quarter)
    e_far = swap(e_out, "span", top)
    cut = comps * lines * 8
    face_sets = jnp.concatenate([e_out[cut:], e_far[cut:]]).reshape(span_count, 8, -1)
    face_blocks = face_blocks + [b ^ top for b in face_blocks]
    e_far = e_far[:cut].reshape(e_own.shape)

    raws, tab, _ = gather(between, f_got, [e_out], quarter, top)
    f_own, f_out = transform(tab, raws, (lines, lines), [], "gathered", comps)
    f_far = swap(f_out, "span", top)
    raws, tab, _ = gather(inner_rows, far_raw, [f_out], top, quarter)
    m_own, m_out = transform(tab, raws, (lines, lines), [e_far], "crossing", comps)
    m_far = swap(m_out, "span", quarter)
    near0 = pl.pallas_call(
        near_kernel,
        grid=grid,
        in_specs=[SMEM, by_wave(state_shape, step), by_wave(side_shape, step), by_wave(side_shape, step), ANY],
        out_specs=by_wave(state_shape, step),
        out_shape=jax.ShapeDtypeStruct(state_shape, jnp.float32),
        scratch_shapes=[pltpu.VMEM(ext_shape, jnp.float32)],
        compiler_params=PARAMS,
        cost_estimate=FREE,
        name="near",
    )(coupling, initial_state, left0, right0, m_out)
    owns, fars = [e_own, f_own, m_own], [e_far, f_far, m_far]
    pieces = len(owns)

    first_shape = (waves, comps, 2, 8, normal)
    ends = pl.pallas_call(
        edge_kernel,
        grid=(2,),
        in_specs=[SMEM]
        + [by_wave2(e_own.shape, waves // 2)] * 2
        + [pl.BlockSpec((waves // 2,) + first_shape[1:], lambda i, n=n: (i, 0, 0, n, 0)) for n in (0, rows // 8 - 1)]
        + [whole(diag.shape), whole(keep.shape), ANY],
        out_specs=by_wave(first_shape, waves // 2),
        out_shape=jax.ShapeDtypeStruct(first_shape, jnp.float32),
        compiler_params=LARGE,
        cost_estimate=FREE,
        name="edge",
    )(speed, e_own, e_far, near0, near0, diag, keep, m_out)
    left1, right1 = halo(ends[:, :, :, :1], ends[:, :, :, 7:], "stream")

    hot = (face_sets[:, :modes, :, None] == jnp.arange(cells * rows, dtype=jnp.float32)).astype(jnp.float32)
    shapes = face_sets[:, modes : 3 * modes].reshape(span_count, modes, 2, -1)
    held = jnp.einsum("bmrf,bmfl->mrbl", shapes, hot, precision=HI).reshape(2 * modes, span_total, rows)
    tab = wave_rows([0], [(b, 0, cells) for b in face_blocks], me, waves, cells, span_total)
    weight = jnp.where(k_mine == 0, 1.0, 2.0).astype(jnp.float32)
    gains = jnp.einsum("mzx,kz->mkx", held, tab, precision=HI).reshape(2 * modes, waves, 2, rows)
    gains = gains * weight[:, None, None]

    step = 4
    grid = (waves // step,)
    flow = pl.pallas_call(
        functools.partial(last_kernel, pieces),
        grid=grid,
        in_specs=[SMEM, SMEM]
        + [by_wave(side_shape, step)] * 2
        + [whole(diag.shape), whole(keep.shape), by_wave(state_shape, step)]
        + [by_wave2(own.shape, step) for own in owns] * 2,
        out_specs=by_wave(state_shape, step),
        out_shape=jax.ShapeDtypeStruct(state_shape, jnp.float32),
        scratch_shapes=[pltpu.VMEM(ext_shape, jnp.float32)],
        compiler_params=LARGE,
        cost_estimate=FREE,
        name="last",
    )(coupling, speed, left1, right1, diag, keep, near0, *owns, *fars)

    wall = flow[:, comps - 1, :, :, 0]
    total = jnp.sum(gains * wall[None], axis=(1, 2, 3)).reshape(modes, 2)
    for axis, count in (("span", span_count), ("stream", stream_count)):
        d = 1
        while d < count:
            total = total + swap(total, axis, d)
            d *= 2
    faces = face_index.shape[1] * stream_count * span_count
    return flow, total / math.sqrt(faces)


def solution(mesh):
    return jax.shard_map(
        shards,
        mesh=mesh,
        in_specs=(
            P(None, "span", "stream", None),
            P("span", None, None, "stream", None),
            P(),
            P(),
            P(),
            P(),
            P(None, ("stream", "span")),
            P(None, None, ("stream", "span")),
        ),
        out_specs=(P("span", None, None, "stream", None), P()),
        check_vma=False,
    )
```

```python
import functools
import math

import jax
import jax.numpy as jnp
from jax import lax
from jax.experimental import pallas as pl
from jax.experimental.pallas import tpu as pltpu
from jax.sharding import PartitionSpec as P

HI = lax.Precision.HIGHEST


def swap(value, axis, dist):
    count = lax.axis_size(axis)
    return lax.ppermute(value, axis, [(i, i ^ dist) for i in range(count)])


def halo(head, tail, axis):
    ends = lax.axis_size(axis) - 1
    left = lax.ppermute(tail, axis, [(i, i + 1) for i in range(ends)])
    right = lax.ppermute(head, axis, [(i + 1, i) for i in range(ends)])
    return left, right


def gate(value, *after):
    return pl.pallas_call(
        lambda *refs: None,
        in_specs=[pl.BlockSpec(memory_space=pl.ANY)] * (1 + len(after)),
        out_specs=pl.BlockSpec(memory_space=pl.ANY),
        out_shape=jax.ShapeDtypeStruct(value.shape, value.dtype),
        input_output_aliases={0: 0},
        cost_estimate=FREE,
        name="gate",
    )(value, *after)


def split_kernel(start, end, faces, after, outer, between):
    @pl.when(pl.program_id(0) < pl.num_programs(0) - 1)
    def _():
        outer[:, :4, :] = start[0, :, :4, :]
        outer[:, 4:, :] = end[0, :, 4:, :]
        between[0, :, :4, :] = end[0, :, :4, :]
        between[0, :, 4:, :] = start[0, :, 4:, :]

    @pl.when(pl.program_id(0) == pl.num_programs(0) - 1)
    def _():
        outer[0] = faces[...]


def split(source, faces, after):
    comps, cells, rows, normal = source.shape
    last = comps - 1

    def spec(tile):
        return pl.BlockSpec((1, cells, 8, normal), lambda c: (jnp.minimum(c, last), 0, tile, 0))

    return pl.pallas_call(
        split_kernel,
        grid=(comps + 1,),
        in_specs=[spec(0), spec(rows // 8 - 1), pl.BlockSpec(faces.shape, lambda c: (0, 0)), ANY],
        out_specs=[pl.BlockSpec((cells, 8, normal), lambda c: (c, 0, 0)), spec(0)],
        out_shape=[
            jax.ShapeDtypeStruct((comps * cells + 1, 8, normal), jnp.float32),
            jax.ShapeDtypeStruct((comps, cells, 8, normal), jnp.float32),
        ],
        compiler_params=PARAMS,
        cost_estimate=FREE,
        name="split",
    )(source, source, faces, after)


def wave_rows(owners, blocks, me, waves, cells, span_total):
    k = (jnp.stack([me ^ d for d in owners])[:, None] * waves + jnp.arange(waves, dtype=jnp.int32)).reshape(-1)
    z = jnp.concatenate([(me ^ d) * cells + start + jnp.arange(size, dtype=jnp.int32) for d, start, size in blocks])
    index = (k[:, None] * z[None, :]) % span_total
    phase = index.astype(jnp.float32) * (2.0 * math.pi / span_total)
    tab = jnp.stack([jnp.cos(phase), -jnp.sin(phase)], axis=1) * (1.0 / math.sqrt(span_total))
    return tab.reshape(len(owners) * waves * 2, z.shape[0])


def halves(value):
    high = value.astype(jnp.bfloat16)
    return high, (value - high.astype(jnp.float32)).astype(jnp.bfloat16)


def table_halves(value):
    high = lax.reduce_precision(value, 8, 7)
    return high.astype(jnp.bfloat16), (value - high).astype(jnp.bfloat16)


def transform_kernel(count, outs_at, sizes, rows, comps, *refs):
    high, low = refs[0], refs[1]
    raws, outs = refs[2 : 2 + count], refs[outs_at:]
    normal = raws[0].shape[-1]
    wide = 2

    @pl.when(pl.program_id(0) < comps)
    def _():
        for x in range(0, rows, wide):
            cols = []
            for j in range(wide):
                cols.append(jnp.concatenate([r[pl.ds(x + j, n, stride=rows), :] for r, n in zip(raws, sizes)], axis=0))
            data = jnp.concatenate(cols, axis=1)
            dh, dl = halves(data)
            dot = functools.partial(jnp.dot, preferred_element_type=jnp.float32)
            val = dot(high[...], dh) + (dot(low[...], dh) + dot(high[...], dl))
            at = 0
            for out in outs:
                lines = out.shape[0] // rows
                for j in range(wide):
                    out[pl.ds(x + j, lines, stride=rows), :] = val[at : at + lines, j * normal : (j + 1) * normal]
                at += lines

    @pl.when(pl.program_id(0) == comps)
    def _():
        for n, raw in enumerate(raws):
            outs[-1][8 * n : 8 * n + 8, :] = raw[:8, :]


def transform(table, raws, lines, after, name, comps, tail=False):
    rows, normal = raws[0].shape[-2:]
    flat = [raw.reshape(-1, normal) for raw in raws]
    sizes = [f.shape[0] // (comps * rows) for f in flat]
    high, low = table_halves(table)
    counts = [comps * n * rows for n in lines]
    if tail:
        counts[-1] += 8 * len(raws)
    first_outs = [pl.BlockSpec((n * rows, normal), lambda c: (jnp.minimum(c, comps - 1), 0)) for n in lines[:-1]]
    outs = pl.pallas_call(
        functools.partial(transform_kernel, len(raws), 2 + len(raws) + len(after), sizes, rows, comps),
        grid=(comps + tail,),
        in_specs=[pl.BlockSpec(table.shape, lambda c: (0, 0))] * 2
        + [pl.BlockSpec((n * rows, normal), lambda c: (c, 0)) for n in sizes]
        + [ANY] * len(after),
        out_specs=first_outs + [pl.BlockSpec((lines[-1] * rows, normal), lambda c: (c, 0))],
        out_shape=[jax.ShapeDtypeStruct((n, normal), jnp.float32) for n in counts],
        compiler_params=PARAMS,
        cost_estimate=FREE,
        name=name,
    )(high, low, *flat, *after)
    return [o if tail and o is outs[-1] else o.reshape(comps, n, rows, normal) for o, n in zip(outs, lines)]


def near_terms(ext, cpl, r, row, comps, normal, wanted):
    lane = lax.broadcasted_iota(jnp.int32, (8, normal), 1)
    parts = []
    for c in range(comps):
        mid = ext[c, r, pl.ds(row, 8), :]
        up = jnp.where(lane < normal - 1, pltpu.roll(mid, normal - 1, 1), 0.0)
        down = jnp.where(lane > 0, pltpu.roll(mid, 1, 1), 0.0)
        parts.append((ext[c, r, pl.ds(row + 1, 8), :], ext[c, r, pl.ds(row - 1, 8), :], up, down))
    out = []
    for c in wanted:
        acc = None
        for e in range(comps):
            for d in range(4):
                term = cpl[d, c, e] * parts[e][d]
                acc = term if acc is None else acc + term
        out.append(acc)
    return out


def near_kernel(cpl, state, left, right, after, near, ext):
    waves, comps, _, rows, normal = state.shape

    def one(k, carry):
        ext[:, :, 8 : 8 + rows, :] = state[k]
        ext[:, :, 7:8, :] = left[k]
        ext[:, :, 8 + rows : 9 + rows, :] = right[k]
        for r in range(2):
            for t in range(rows // 8):
                sums = near_terms(ext, cpl, r, 8 + 8 * t, comps, normal, range(comps))
                for c in range(comps):
                    near[k, c, r, 8 * t : 8 * t + 8, :] = sums[c]
        return carry

    lax.fori_loop(0, waves, one, 0)


def rotate(re, im, a, b, keep):
    scale = keep / (a * a + b * b)
    return (a * re + b * im) * scale, (a * im - b * re) * scale


def edge_kernel(speed, own, far, near_start, near_end, diag, keep, after, first):
    waves, comps, _, _, normal = near_start.shape
    rows = keep.shape[0]
    base = pl.program_id(0) * waves
    low = lax.broadcasted_iota(jnp.int32, (8, normal), 0) < 4

    def one(k, carry):
        for c in range(comps):
            defect = []
            for r in range(2):
                old = jnp.where(low, near_start[k, c, r], near_end[k, c, r])
                defect.append(own[c, 2 * k + r] + far[c, 2 * k + r] - old)
            a = jnp.where(low, diag[c, :8, :], diag[c, rows - 8 :, :])
            out = rotate(*defect, a, speed[base + k, c], jnp.where(low, keep[:8, :], keep[rows - 8 :, :]))
            first[k, c, 0], first[k, c, 1] = out
        return carry

    lax.fori_loop(0, waves, one, 0)


def tile_sums(owns, fars, low, rows, c, at):
    outer, between, middle = [own[c, at] + far[c, at] for own, far in zip(owns, fars)]
    middle = [middle[t : t + 8] for t in range(0, rows - 16, 8)]
    return [jnp.where(low, outer, between)] + middle + [jnp.where(low, between, outer)]


def last_kernel(pieces, cpl, speed, left, right, diag, keep, near, *rest):
    owns, fars = rest[:pieces], rest[pieces : 2 * pieces]
    flow, ext = rest[2 * pieces :]
    waves, comps, _, rows, normal = flow.shape
    base = pl.program_id(0) * waves
    low = lax.broadcasted_iota(jnp.int32, (8, normal), 0) < 4

    def one(k, carry):
        ext[:, :, 7:8, :] = left[k]
        ext[:, :, 8 + rows : 9 + rows, :] = right[k]
        for c in range(comps):
            b = speed[base + k, c]
            rhs = [tile_sums(owns, fars, low, rows, c, 2 * k + r) for r in range(2)]
            for n in range(rows // 8):
                src = slice(8 * n, 8 * n + 8)
                re, im = (rhs[r][n] - near[k, c, r, src, :] for r in range(2))
                re, im = rotate(re, im, diag[c, src, :], b, keep[src, :])
                ext[c, 0, 8 + 8 * n : 16 + 8 * n, :], ext[c, 1, 8 + 8 * n : 16 + 8 * n, :] = re, im
                flow[k, c, 0, src, :], flow[k, c, 1, src, :] = rhs[0][n], rhs[1][n]
        for n in range(rows // 8):
            src = slice(8 * n, 8 * n + 8)
            sums = [near_terms(ext, cpl, r, 8 + 8 * n, comps, normal, range(comps)) for r in range(2)]
            for c in range(comps):
                re, im = (flow[k, c, r, src, :] - sums[r][c] for r in range(2))
                out = rotate(re, im, diag[c, src, :], speed[base + k, c], keep[src, :])
                flow[k, c, 0, src, :], flow[k, c, 1, src, :] = out
        return carry

    lax.fori_loop(0, waves, one, 0)


def by_wave(shape, step, skip=0):
    rest = len(shape) - 1
    return pl.BlockSpec((step,) + tuple(shape[1:]), lambda i: (i + skip,) + (0,) * rest)


def by_wave2(shape, step, skip=0):
    return pl.BlockSpec((shape[0], 2 * step) + tuple(shape[2:]), lambda i: (0, i + skip, 0, 0))


def whole(shape):
    return pl.BlockSpec(tuple(shape), lambda i: (0,) * len(shape))


SMEM = pl.BlockSpec(memory_space=pltpu.SMEM)
ANY = pl.BlockSpec(memory_space=pl.ANY)
LARGE = pltpu.CompilerParams(vmem_limit_bytes=60 * 1024 * 1024)
PARAMS = pltpu.CompilerParams(vmem_limit_bytes=48 * 1024 * 1024)


FREE = pl.CostEstimate(flops=0, bytes_accessed=0, transcendentals=0)


def shards(forcing, initial_state, diagonal, span_speed, coupling, stiffener_mask, face_index, mode_shapes):
    span_count = lax.axis_size("span")
    stream_count = lax.axis_size("stream")
    me = lax.axis_index("span")
    comps, cells, rows, normal = forcing.shape
    waves = initial_state.shape[0]
    span_total = cells * span_count
    half_span = span_count // 2
    modes = face_index.shape[0]
    inner = [d for d in (1 << i for i in range(20)) if d < half_span]

    k_mine = me * waves + jnp.arange(waves, dtype=jnp.int32)
    first_cell = lax.axis_index("stream") * rows
    keep = lax.dynamic_slice_in_dim((1 - stiffener_mask).astype(jnp.float32), first_cell, rows, 0)
    diag = lax.dynamic_slice_in_dim(diagonal, first_cell, rows, 1)
    speed = (k_mine.astype(jnp.float32) * (2.0 * math.pi / span_total))[:, None] * span_speed[None, :]
    left0, right0 = halo(initial_state[:, :, :, :1], initial_state[:, :, :, rows - 1 :], "stream")
    step = 4
    grid = (waves // step,)
    state_shape = initial_state.shape
    side_shape = left0.shape
    ext_shape = (comps, 2, rows + 16, normal)
    top, quarter = half_span, half_span // 2
    lower = [d for d in reversed(inner) if d < quarter]
    faces = [face_index.astype(jnp.float32), mode_shapes.reshape(2 * modes, -1)]
    faces = jnp.concatenate(faces + [jnp.zeros((8 - 3 * modes, face_index.shape[1]), jnp.float32)], axis=0)
    inner_rows = forcing[:, :, 8 : rows - 8]
    far_raw = swap(inner_rows, "span", half_span)
    outer, between = split(forcing, faces, inner_rows)

    def gather(raw, got, hold, first, last):
        late = gate(got, *hold) if hold else got
        sets = [(raw, 0, 0), (late, first, 0)]
        for d in lower:
            more = []
            for value, block, start in sets:
                cuts = 4 if block & first and value.shape[1] == cells and value.ndim == 4 else 1
                size = value.shape[1] // cuts if value.ndim == 4 else cells
                for n in range(cuts):
                    part = value[:, n * size : (n + 1) * size] if cuts > 1 else value
                    more.append((swap(part, "span", d), block ^ d, start + n * size))
            sets = sets + more
        blocks = [(block, start, value.shape[1] if value.ndim == 4 else cells) for value, block, start in sets]
        return [value for value, _, _ in sets], wave_rows([0, last], blocks, me, waves, cells, span_total), [b for b, _, _ in blocks]

    e_got = swap(outer, "span", quarter)
    raws, tab, face_blocks = gather(outer, e_got, [], quarter, top)
    lines = 2 * waves
    e_own, e_out = transform(tab, raws, (lines, lines), [keep, diag, speed, left0, right0], "gathered", comps, True)
    f_got = swap(gate(between, e_got), "span", quarter)
    e_far = swap(e_out, "span", top)
    cut = comps * lines * 8
    face_sets = jnp.concatenate([e_out[cut:], e_far[cut:]]).reshape(span_count, 8, -1)
    face_blocks = face_blocks + [b ^ top for b in face_blocks]
    e_far = e_far[:cut].reshape(e_own.shape)

    near0 = pl.pallas_call(
        near_kernel,
        grid=grid,
        in_specs=[SMEM, by_wave(state_shape, step), by_wave(side_shape, step), by_wave(side_shape, step), ANY],
        out_specs=by_wave(state_shape, step),
        out_shape=jax.ShapeDtypeStruct(state_shape, jnp.float32),
        scratch_shapes=[pltpu.VMEM(ext_shape, jnp.float32)],
        compiler_params=PARAMS,
        cost_estimate=FREE,
        name="near",
    )(coupling, initial_state, left0, right0, e_out)
    raws, tab, _ = gather(between, f_got, [near0], quarter, top)
    f_own, f_out = transform(tab, raws, (lines, lines), [], "gathered", comps)
    f_far = swap(f_out, "span", top)
    raws, tab, _ = gather(inner_rows, far_raw, [f_out], top, quarter)
    m_own, m_out = transform(tab, raws, (lines, lines), [e_far], "crossing", comps)
    m_far = swap(m_out, "span", quarter)
    owns, fars = [e_own, f_own, m_own], [e_far, f_far, m_far]
    pieces = len(owns)

    first_shape = (waves, comps, 2, 8, normal)
    ends = pl.pallas_call(
        edge_kernel,
        grid=(2,),
        in_specs=[SMEM]
        + [by_wave2(e_own.shape, waves // 2)] * 2
        + [pl.BlockSpec((waves // 2,) + first_shape[1:], lambda i, n=n: (i, 0, 0, n, 0)) for n in (0, rows // 8 - 1)]
        + [whole(diag.shape), whole(keep.shape), ANY],
        out_specs=by_wave(first_shape, waves // 2),
        out_shape=jax.ShapeDtypeStruct(first_shape, jnp.float32),
        compiler_params=LARGE,
        cost_estimate=FREE,
        name="edge",
    )(speed, e_own, e_far, near0, near0, diag, keep, m_out)
    left1, right1 = halo(ends[:, :, :, :1], ends[:, :, :, 7:], "stream")

    hot = (face_sets[:, :modes, :, None] == jnp.arange(cells * rows, dtype=jnp.float32)).astype(jnp.float32)
    shapes = face_sets[:, modes : 3 * modes].reshape(span_count, modes, 2, -1)
    held = jnp.einsum("bmrf,bmfl->mrbl", shapes, hot, precision=HI).reshape(2 * modes, span_total, rows)
    tab = wave_rows([0], [(b, 0, cells) for b in face_blocks], me, waves, cells, span_total)
    weight = jnp.where(k_mine == 0, 1.0, 2.0).astype(jnp.float32)
    gains = jnp.einsum("mzx,kz->mkx", held, tab, precision=HI).reshape(2 * modes, waves, 2, rows)
    gains = gains * weight[:, None, None]

    step = 4
    grid = (waves // step,)
    flow = pl.pallas_call(
        functools.partial(last_kernel, pieces),
        grid=grid,
        in_specs=[SMEM, SMEM]
        + [by_wave(side_shape, step)] * 2
        + [whole(diag.shape), whole(keep.shape), by_wave(state_shape, step)]
        + [by_wave2(own.shape, step) for own in owns] * 2,
        out_specs=by_wave(state_shape, step),
        out_shape=jax.ShapeDtypeStruct(state_shape, jnp.float32),
        scratch_shapes=[pltpu.VMEM(ext_shape, jnp.float32)],
        compiler_params=LARGE,
        cost_estimate=FREE,
        name="last",
    )(coupling, speed, left1, right1, diag, keep, near0, *owns, *fars)

    wall = flow[:, comps - 1, :, :, 0]
    total = jnp.sum(gains * wall[None], axis=(1, 2, 3)).reshape(modes, 2)
    for axis, count in (("span", span_count), ("stream", stream_count)):
        d = 1
        while d < count:
            total = total + swap(total, axis, d)
            d *= 2
    faces = face_index.shape[1] * stream_count * span_count
    return flow, total / math.sqrt(faces)


def solution(mesh):
    return jax.shard_map(
        shards,
        mesh=mesh,
        in_specs=(
            P(None, "span", "stream", None),
            P("span", None, None, "stream", None),
            P(),
            P(),
            P(),
            P(),
            P(None, ("stream", "span")),
            P(None, None, ("stream", "span")),
        ),
        out_specs=(P("span", None, None, "stream", None), P()),
        check_vma=False,
    )
```
